32 devices in a mesh: blk: 8 (over z, x), rep: 4 (over y, core).
Axes of the slice: x: 2, y: 2, z: 4, core: 2. Of those that a mesh axis runs over, the one named last changes fastest.
Arguments:
- features: bfloat16 [8192, 256], P(('blk', 'rep')), may hold values from -6 to 6
- weight: bfloat16 [256, 256], replicated, may hold values from -0.375 to 0.375
- pre_cot: bfloat16 [8192, 256], P(('blk', 'rep')), may hold values from -6 to 6
- tile_count: int32 [8, 4, 8], P('blk', 'rep'), may hold values from 0 to 2, as said below
- tile_rowid: int32 [8, 4, 8, 2], P('blk', 'rep'), may hold values from 0 to 3, as said below
- edge_cols: int32 [8, 4, 8, 2, 1, 256], P('blk', 'rep'), may hold values from 0 to 255
- edge_vals: bfloat16 [8, 4, 8, 2, 1, 256], P('blk', 'rep'), may hold values from -1.25 to 1.25
Outputs:
- activations: bfloat16 [8192, 256], P(('blk', 'rep'))
- grad_weight: float32 [256, 256], replicated
The draws below stay inside these ranges and needn't reach their ends.
Inputs may be any that keep to these rules, and one draw needn't show every extreme that they name: `tile_count`: the panel p = b always has all 2 slots live. `tile_rowid`: the 2 slots of one block row, tile position and panel name distinct row tiles.
All inputs are finite; a program needn't handle non-finite values.
Results may differ from the reference program's by a relative error of at most 0.011.
Values may be sent and summed in bfloat16 or wider, within the bound.
A program may use at most 64 MiB of HBM per device.

```python
import jax
import jax.numpy as jnp
from jax import lax

F = 256
TILE = 256
DEG = 1
SLOTS = 2
ROWS_BLK = 1024
NODES = 8192
N_BLK = 8
N_REP = 4


def draw_tile_count(key, part):
    key_cap, key_draw = jax.random.split(key)
    row_cap = jax.random.randint(key_cap, (N_BLK, 1, 1), 1, SLOTS + 1)
    counts = jax.random.randint(key_draw, (N_BLK, N_REP, N_BLK), 0, row_cap + 1)
    diagonal = lax.broadcasted_iota(jnp.int32, (N_BLK, N_REP, N_BLK), 0) == lax.broadcasted_iota(jnp.int32, (N_BLK, N_REP, N_BLK), 2)
    return jnp.where(diagonal, SLOTS, counts).astype(jnp.int32)


def draw_tile_rowid(key, part):
    shape_all = (N_BLK, N_REP, N_BLK, N_REP)
    scores = jax.random.randint(key, shape_all, 0, 1 << 20)
    scores = scores * N_REP + lax.broadcasted_iota(jnp.int32, shape_all, 3)
    order = jnp.argsort(scores, axis=-1, stable=True)
    return order[..., :SLOTS].astype(jnp.int32)


def draw_edge_cols(key, part):
    shape_all = (N_BLK, N_REP, N_BLK, SLOTS, DEG, TILE)
    return jax.random.randint(key, shape_all, 0, TILE).astype(jnp.int32)


def shard_levels(key, shape, pieces, least, high):
    gain = 1.0
    for dim, blocks in pieces:
        steps = jax.random.uniform(jax.random.fold_in(jax.random.fold_in(key, 6), dim), (blocks,), jnp.float32, least / len(pieces), high / len(pieces))
        gain = gain * jnp.repeat(jnp.exp(steps), shape[dim] // blocks).reshape((-1,) + (1,) * (len(shape) - 1 - dim))
    return gain


def centred(stream_key, shape, deviation, limit, pieces=(), kind=jnp.bfloat16):
    values = deviation * jax.random.normal(stream_key, shape, jnp.float32)
    if pieces:
        values = values * shard_levels(stream_key, shape, pieces, -0.22, 0.18)
    return jnp.clip(values, -limit, limit).astype(kind)


def setup_inputs(seed: int = 0) -> dict:
    arg_keys = jax.random.split(jax.random.key(seed), 8)
    features = centred(arg_keys[0], (NODES, F), 1.0, 6.0, ((0, 32),))
    weight = centred(arg_keys[1], (F, F), F ** -0.5, 0.375)
    pre_cot = centred(arg_keys[2], (NODES, F), 1.0, 6.0, ((0, 32),))
    tile_count = draw_tile_count(jax.random.fold_in(arg_keys[7], 71), 0)
    tile_rowid = draw_tile_rowid(jax.random.fold_in(arg_keys[7], 71), 0)
    edge_cols = draw_edge_cols(jax.random.fold_in(arg_keys[7], 71), 0)
    edge_vals = centred(arg_keys[6], (N_BLK, N_REP, N_BLK, SLOTS, DEG, TILE), 0.2, 1.25, ((0, 8), (1, 4)))
    return {"features": features, "weight": weight, "pre_cot": pre_cot, "tile_count": tile_count, "tile_rowid": tile_rowid, "edge_cols": edge_cols, "edge_vals": edge_vals}


def reference(features, weight, pre_cot, tile_count, tile_rowid, edge_cols, edge_vals):
    feat_tiles = features.reshape(N_BLK, N_REP, TILE, F)
    slot_ids = jnp.arange(SLOTS, dtype=jnp.int32)
    tile_ids = jnp.arange(N_REP, dtype=jnp.int32)

    def block_row(block):
        def column_tile(column):
            def panel_step(totals, panel):
                source = feat_tiles[panel, column].astype(jnp.float32)
                index_now = edge_cols[block, column, panel]
                weight_now = edge_vals[block, column, panel].astype(jnp.float32)
                sums = jnp.zeros((SLOTS, TILE, F), jnp.float32)
                for degree in range(DEG):
                    sums = sums + weight_now[:, degree, :, None] * source[index_now[:, degree, :]]
                live_mask = (slot_ids < tile_count[block, column, panel]).astype(jnp.float32)
                placing = (tile_rowid[block, column, panel][:, None] == tile_ids[None, :]).astype(jnp.float32)
                placing = placing * live_mask[:, None]
                totals = totals + jnp.einsum("sn,sif->nif", placing, sums, precision=lax.Precision.HIGHEST)
                return totals, None

            totals, _ = lax.scan(panel_step, jnp.zeros((N_REP, TILE, F), jnp.float32),
                                 jnp.arange(N_BLK, dtype=jnp.int32))
            return totals.astype(jnp.bfloat16)

        partials = lax.map(column_tile, jnp.arange(N_REP, dtype=jnp.int32))
        partials = lax.optimization_barrier(partials)
        summed = jnp.sum(partials.astype(jnp.float32), axis=0)
        return summed.reshape(ROWS_BLK, F).astype(jnp.bfloat16)

    aggregate = lax.map(block_row, jnp.arange(N_BLK, dtype=jnp.int32)).reshape(NODES, F)
    preact = jnp.dot(aggregate, weight, preferred_element_type=jnp.float32)
    activations = jnp.maximum(preact, 0.0).astype(jnp.bfloat16)
    grad_weight = jnp.dot(aggregate.T, pre_cot, preferred_element_type=jnp.float32) * (NODES ** -0.5)
    return activations, grad_weight
```

```python
import functools

import jax
import jax.numpy as jnp
from jax import lax
from jax.experimental import pallas as pl
from jax.experimental.pallas import tpu as pltpu
from jax.sharding import PartitionSpec as P


def shifted(array, axis, by):
    count = lax.axis_size(axis)
    return lax.ppermute(array, axis, [(i, (i + by) % count) for i in range(count)])


def shards(features, weight, pre_cot, tile_count, tile_rowid, edge_cols, edge_vals):
    tile_rows = features.shape[0]
    feat_width = features.shape[1]
    rep_count = lax.axis_size("rep")
    blocks = lax.axis_size("blk")
    home_index = lax.axis_index("blk")
    counts = tile_count.reshape(-1)
    row_ids = tile_rowid.reshape(tile_rowid.shape[2], tile_rowid.shape[3])
    edge_index = edge_cols.reshape(edge_cols.shape[2:])
    edge_weight = edge_vals.reshape(edge_vals.shape[2:])
    slot_count = edge_index.shape[1]
    columns = lax.broadcasted_iota(jnp.int32, (1, 1, 1, tile_rows), 3)
    slot_ids = jnp.arange(slot_count, dtype=jnp.int32)
    zero_weight = jnp.zeros((), jnp.bfloat16)
    totals_start = jnp.zeros((rep_count * tile_rows, feat_width), jnp.float32)

    def apply_panel(totals, panel_now, panel_index):
        index_now = lax.dynamic_index_in_dim(edge_index, panel_index, 0, keepdims=False)
        weight_now = lax.dynamic_index_in_dim(edge_weight, panel_index, 0, keepdims=False)
        dense_tiles = jnp.sum(
            jnp.where(index_now[..., None] == columns, weight_now[..., None], zero_weight), axis=1
        )
        products = jnp.einsum(
            "sij,jf->sif", dense_tiles, panel_now, preferred_element_type=jnp.float32
        )
        live_mask = (slot_ids < counts[panel_index]).astype(jnp.float32)
        slot_rows = lax.dynamic_index_in_dim(row_ids, panel_index, 0, keepdims=False)
        for slot in range(slot_count):
            row_start = slot_rows[slot] * tile_rows
            current = lax.dynamic_slice_in_dim(totals, row_start, tile_rows, 0)
            totals = lax.dynamic_update_slice_in_dim(
                totals, current + products[slot] * live_mask[slot], row_start, 0
            )
        return totals

    totals = apply_panel(totals_start, features, home_index)

    def cycle_turn(turn_index, carry):
        totals_now, panel_now = carry
        panel_now = shifted(panel_now, "blk", 1)
        totals_now = apply_panel(totals_now, panel_now, (home_index - turn_index) % blocks)
        return (totals_now, panel_now)

    totals, _ = lax.fori_loop(1, blocks, cycle_turn, (totals, features))
    summed = lax.psum_scatter(totals.astype(jnp.bfloat16), "rep", scatter_dimension=0, tiled=True)
    preact = jnp.dot(summed, weight, preferred_element_type=jnp.float32)
    activations = jnp.maximum(preact, 0.0).astype(jnp.bfloat16)
    local_grad = lax.dot_general(
        summed, pre_cot, (((0,), (0,)), ((), ())), preferred_element_type=jnp.float32
    )
    total_grad = lax.psum(local_grad, ("blk", "rep"))
    node_total = blocks * rep_count * tile_rows
    grad_weight = total_grad * node_total ** (-0.5)
    return (activations, grad_weight)


MESH = pl.DeviceIdType.MESH
CHUNKS = 1


def fits(mesh):
    blocks, reps = mesh.shape["blk"], mesh.shape["rep"]
    return blocks % 2 == 0 and blocks * reps <= 32


def kernel(blocks, reps, chunks, scale, feat, weight, pre, count, rowid, cols, vals, act, grad,
           onehot, panels, pres, total, part, part_in, s1, r1, s2, r2, r3, r4,
           x_send, x_recv, pre_send, pre_recv, p_send, p_recv,
           g1_send, g1_recv, g2_send, g2_recv, g3_send, g3_recv, g4_send, g4_recv):
    blk, rep = lax.axis_index("blk"), lax.axis_index("rep")
    tile, width = feat.shape
    part_width = width // chunks
    depth = blocks // 2
    x, z = lax.rem(blk, 2), blk // 2

    barrier = pltpu.get_barrier_semaphore()
    for k in range(1, blocks):
        pl.semaphore_signal(barrier, inc=1, device_id=(lax.rem(blk + k, blocks), rep), device_id_type=MESH)
    for k in range(1, reps):
        pl.semaphore_signal(barrier, inc=1, device_id=(blk, lax.rem(rep + k, reps)), device_id_type=MESH)
    for c in range(chunks):
        panels[c, blk] = feat[:, c * part_width:(c + 1) * part_width]
    pl.semaphore_wait(barrier, blocks + reps - 2)

    def remote(src, dst, send, recv, to):
        return pltpu.make_async_remote_copy(
            src_ref=src, dst_ref=dst, send_sem=send, recv_sem=recv, device_id=to, device_id_type=MESH
        )

    targets = (blk + 2, blk - 2, blk + 1 - 2 * x)

    def panel_copy(c, slot, way):
        to = targets[way]
        return remote(panels.at[c, slot], panels.at[c, slot], x_send.at[c, slot, way],
                      x_recv.at[c, slot], (to, rep))

    def order(k):
        low = jnp.minimum(z, depth - 1 - z)
        half = (k + 1) // 2
        near = z - half if k % 2 == 1 else z + half
        far = jnp.where(z < depth - 1 - z, z + (k - low), z - (k - low))
        return jnp.where(k <= 2 * low, near, far)

    def own(c):
        pl.when(z + 1 < depth)(lambda: panel_copy(c, blk, 0).start())
        pl.when(z > 0)(lambda: panel_copy(c, blk, 1).start())
        panel_copy(c, blk, 2).start()

    def build(p, carry):
        rows = lax.broadcasted_iota(jnp.int32, (tile, tile), 0)
        live = count[0, 0, p]
        c0, c1 = cols[0, 0, p, 0], cols[0, 0, p, 1]
        v0, v1 = vals[0, 0, p, 0].astype(jnp.float32), vals[0, 0, p, 1].astype(jnp.float32)
        for t in range(reps):
            first = jnp.logical_and(rowid[0, 0, p, 0] == t, live > 0)
            second = jnp.logical_and(rowid[0, 0, p, 1] == t, live > 1)
            value = jnp.where(first, v0, jnp.where(second, v1, 0.0))
            index = jnp.where(first, c0, c1)
            onehot[p, :, t * tile:(t + 1) * tile] = jnp.where(rows == index, value, 0.0).astype(jnp.bfloat16)
        return carry

    def product(c, slot):
        return lax.dot_general(panels[c, slot], onehot[slot], (((0,), (0,)), ((), ())),
                               preferred_element_type=jnp.float32)

    def take(c, slot):
        total[c] += product(c, slot)

    def arrive(c, slot):
        panel_copy(c, slot, 2).wait_recv()

    def step(c, k):
        where = order(k)
        slot = where * 2 + x
        arrive(c, slot)
        pl.when(jnp.logical_and(where < z, z + 1 < depth))(lambda: panel_copy(c, slot, 0).start())
        pl.when(jnp.logical_and(where > z, z > 0))(lambda: panel_copy(c, slot, 1).start())
        panel_copy(c, slot, 2).start()
        take(c, slot)
        last = (z if k == 1 else order(k - 1)) * 2 + 1 - x
        arrive(c, last)
        take(c, last)

    def to_rep(src, dst, send, recv, k):
        return remote(src, dst, send.at[k], recv.at[rep], (blk, lax.rem(rep + k, reps)))

    def from_rep(dst, send, recv, k):
        source = lax.rem(rep + k, reps)
        remote(dst.at[source], dst.at[source], send.at[k], recv.at[source], (blk, source)).wait_recv()
        return source

    def pre_copy(k):
        return to_rep(pre, pres.at[rep], pre_send, pre_recv, k)

    def part_copy(c, k):
        return to_rep(part.at[c, lax.rem(rep + k, reps)], part_in.at[c, rep], p_send.at[c], p_recv.at[c], k)

    own(0)
    for k in range(1, reps):
        pre_copy(k).start()
    pres[rep] = pre[...]
    lax.fori_loop(0, blocks, build, 0)

    grad_rows = []
    for c in range(chunks):
        if c:
            own(c)
        total[c] = product(c, blk)
        for k in range(1, depth):
            step(c, k)
        last = order(depth - 1) * 2 + 1 - x
        arrive(c, last)
        take(c, last)
        for t in range(reps):
            part[c, t] = total[c, :, t * tile:(t + 1) * tile].astype(jnp.bfloat16)
        if c == 0:
            for k in range(1, reps):
                from_rep(pres, pre_send, pre_recv, k)
        rows = jnp.dot(part[c, 0], pres[0], preferred_element_type=jnp.float32)
        for t in range(1, reps):
            rows += jnp.dot(part[c, t], pres[t], preferred_element_type=jnp.float32)
        share = width // reps
        for q in range(part_width // share):
            s1[c * (part_width // share) + q] = rows[q * share:(q + 1) * share]
        if c < chunks - 1:
            for k in range(1, reps):
                part_copy(c, k).start()

    share = width // reps

    def g1_copy(k):
        return to_rep(r1.at[reps + lax.rem(rep + k, reps)], r1.at[rep], g1_send, g1_recv, k)

    for q in range(reps):
        r1[reps + q] = s1[q].astype(jnp.bfloat16)
    for k in range(1, reps):
        g1_copy(k).start()
    for k in range(1, reps):
        part_copy(chunks - 1, k).start()

    mine = s1[rep]
    for k in range(1, reps):
        mine += r1[from_rep(r1, g1_send, g1_recv, k)].astype(jnp.float32)
    piece = share * width // blocks // 128
    lanes = width // 128
    for k in range(blocks):
        s2[k] = mine[(k // lanes) * piece:(k // lanes + 1) * piece,
                     (k % lanes) * 128:(k % lanes + 1) * 128].astype(jnp.bfloat16)

    def to_blk(src, dst, send, recv, k):
        return remote(src, dst, send.at[k], recv.at[blk], (lax.rem(blk + k, blocks), rep))

    def from_blk(dst, send, recv, k):
        source = lax.rem(blk + k, blocks)
        remote(dst.at[source], dst.at[source], send.at[k], recv.at[source], (source, rep)).wait_recv()
        return source

    def g2_copy(k):
        return to_blk(s2.at[lax.rem(blk + k, blocks)], r2.at[blk], g2_send, g2_recv, k)

    for k in range(1, blocks):
        g2_copy(k).start()
    summed = s2[blk].astype(jnp.float32)
    for k in range(1, blocks):
        summed += r2[from_blk(r2, g2_send, g2_recv, k)].astype(jnp.float32)
    r3[blk] = (summed * scale).astype(jnp.bfloat16)

    def g3_copy(k):
        return to_blk(r3.at[blk], r3.at[blk], g3_send, g3_recv, k)

    for k in range(1, blocks):
        g3_copy(k).start()

    preact = jnp.zeros((tile, width), jnp.float32)
    for c in range(chunks):
        node = part[c, rep].astype(jnp.float32)
        for k in range(1, reps):
            node += part_in[c, from_rep(part_in.at[c], p_send.at[c], p_recv.at[c], k)].astype(jnp.float32)
        preact += lax.dot_general(node.astype(jnp.bfloat16), weight[c * part_width:(c + 1) * part_width],
                                  (((0,), (0,)), ((), ())), preferred_element_type=jnp.float32)
    act[...] = jnp.maximum(preact, 0.0).astype(jnp.bfloat16)

    for k in range(1, blocks):
        from_blk(r3, g3_send, g3_recv, k)

    def g4_copy(k):
        return to_rep(r3, r4.at[rep], g4_send, g4_recv, k)

    for k in range(1, reps):
        g4_copy(k).start()
    r4[rep] = r3[...]
    for c in range(chunks):
        pl.when(z + 1 < depth)(lambda: panel_copy(c, blk, 0).wait_send())
        pl.when(z > 0)(lambda: panel_copy(c, blk, 1).wait_send())
        panel_copy(c, blk, 2).wait_send()
        for k in range(1, depth):
            where = order(k)
            slot = where * 2 + x
            pl.when(jnp.logical_and(where < z, z + 1 < depth))(lambda: panel_copy(c, slot, 0).wait_send())
            pl.when(jnp.logical_and(where > z, z > 0))(lambda: panel_copy(c, slot, 1).wait_send())
            panel_copy(c, slot, 2).wait_send()
        for k in range(1, reps):
            part_copy(c, k).wait_send()
    for k in range(1, reps):
        pre_copy(k).wait_send()
        g1_copy(k).wait_send()
    for k in range(1, blocks):
        g2_copy(k).wait_send()
        g3_copy(k).wait_send()
    for k in range(1, reps):
        from_rep(r4, g4_send, g4_recv, k)
    for q in range(reps):
        for k in range(blocks):
            row = q * share + (k // lanes) * piece
            grad[row:row + piece, (k % lanes) * 128:(k % lanes + 1) * 128] = r4[q, k].astype(jnp.float32)
    for k in range(1, reps):
        g4_copy(k).wait_send()


def fused(features, weight, pre_cot, tile_count, tile_rowid, edge_cols, edge_vals):
    blocks, reps = lax.axis_size("blk"), lax.axis_size("rep")
    tile, width = features.shape
    chunks, part_width = CHUNKS, width // CHUNKS
    share = width // reps
    piece = share * width // blocks // 128
    dma = pltpu.SemaphoreType.DMA
    vmem = pl.BlockSpec(memory_space=pltpu.VMEM)
    smem = pl.BlockSpec(memory_space=pltpu.SMEM)
    bf16 = jnp.bfloat16
    scale = (blocks * reps * tile) ** (-0.5)
    return pl.pallas_call(
        functools.partial(kernel, blocks, reps, chunks, scale),
        out_shape=(jax.ShapeDtypeStruct((tile, width), bf16), jax.ShapeDtypeStruct((width, width), jnp.float32)),
        in_specs=[vmem, vmem, vmem, smem, smem, vmem, vmem],
        out_specs=(vmem, vmem),
        scratch_shapes=[
            pltpu.VMEM((blocks, tile, reps * tile), bf16),
            pltpu.VMEM((chunks, blocks, tile, part_width), bf16),
            pltpu.VMEM((reps, tile, width), bf16),
            pltpu.VMEM((chunks, part_width, reps * tile), jnp.float32),
            pltpu.VMEM((chunks, reps, part_width, tile), bf16),
            pltpu.VMEM((chunks, reps, part_width, tile), bf16),
            pltpu.VMEM((reps, share, width), jnp.float32),
            pltpu.VMEM((2 * reps, share, width), bf16),
            pltpu.VMEM((blocks, piece, 128), bf16),
            pltpu.VMEM((blocks, piece, 128), bf16),
            pltpu.VMEM((blocks, piece, 128), bf16),
            pltpu.VMEM((reps, blocks, piece, 128), bf16),
            dma((chunks, blocks, 3)), dma((chunks, blocks)), dma((reps,)), dma((reps,)),
            dma((chunks, reps)), dma((chunks, reps)),
            dma((reps,)), dma((reps,)), dma((blocks,)), dma((blocks,)),
            dma((blocks,)), dma((blocks,)), dma((reps,)), dma((reps,)),
        ],
        compiler_params=pltpu.CompilerParams(
            collective_id=0, has_side_effects=True, vmem_limit_bytes=40 * 1024 * 1024
        ),
    )(features, weight, pre_cot, tile_count, tile_rowid, edge_cols, edge_vals)


def solution(mesh):
    in_specs = (
        P(("blk", "rep"), None),
        P(),
        P(("blk", "rep"), None),
        P("blk", "rep", None),
        P("blk", "rep", None, None),
        P("blk", "rep", None, None, None, None),
        P("blk", "rep", None, None, None, None),
    )
    out_specs = (P(("blk", "rep"), None), P())
    body = fused if fits(mesh) else shards
    return jax.shard_map(body, mesh=mesh, in_specs=in_specs, out_specs=out_specs, check_vma=False)
```

```python
import functools

import jax
import jax.numpy as jnp
from jax import lax
from jax.experimental import pallas as pl
from jax.experimental.pallas import tpu as pltpu
from jax.sharding import PartitionSpec as P


def shifted(array, axis, by):
    count = lax.axis_size(axis)
    return lax.ppermute(array, axis, [(i, (i + by) % count) for i in range(count)])


def shards(features, weight, pre_cot, tile_count, tile_rowid, edge_cols, edge_vals):
    tile_rows = features.shape[0]
    feat_width = features.shape[1]
    rep_count = lax.axis_size("rep")
    blocks = lax.axis_size("blk")
    home_index = lax.axis_index("blk")
    counts = tile_count.reshape(-1)
    row_ids = tile_rowid.reshape(tile_rowid.shape[2], tile_rowid.shape[3])
    edge_index = edge_cols.reshape(edge_cols.shape[2:])
    edge_weight = edge_vals.reshape(edge_vals.shape[2:])
    slot_count = edge_index.shape[1]
    columns = lax.broadcasted_iota(jnp.int32, (1, 1, 1, tile_rows), 3)
    slot_ids = jnp.arange(slot_count, dtype=jnp.int32)
    zero_weight = jnp.zeros((), jnp.bfloat16)
    totals_start = jnp.zeros((rep_count * tile_rows, feat_width), jnp.float32)

    def apply_panel(totals, panel_now, panel_index):
        index_now = lax.dynamic_index_in_dim(edge_index, panel_index, 0, keepdims=False)
        weight_now = lax.dynamic_index_in_dim(edge_weight, panel_index, 0, keepdims=False)
        dense_tiles = jnp.sum(
            jnp.where(index_now[..., None] == columns, weight_now[..., None], zero_weight), axis=1
        )
        products = jnp.einsum(
            "sij,jf->sif", dense_tiles, panel_now, preferred_element_type=jnp.float32
        )
        live_mask = (slot_ids < counts[panel_index]).astype(jnp.float32)
        slot_rows = lax.dynamic_index_in_dim(row_ids, panel_index, 0, keepdims=False)
        for slot in range(slot_count):
            row_start = slot_rows[slot] * tile_rows
            current = lax.dynamic_slice_in_dim(totals, row_start, tile_rows, 0)
            totals = lax.dynamic_update_slice_in_dim(
                totals, current + products[slot] * live_mask[slot], row_start, 0
            )
        return totals

    totals = apply_panel(totals_start, features, home_index)

    def cycle_turn(turn_index, carry):
        totals_now, panel_now = carry
        panel_now = shifted(panel_now, "blk", 1)
        totals_now = apply_panel(totals_now, panel_now, (home_index - turn_index) % blocks)
        return (totals_now, panel_now)

    totals, _ = lax.fori_loop(1, blocks, cycle_turn, (totals, features))
    summed = lax.psum_scatter(totals.astype(jnp.bfloat16), "rep", scatter_dimension=0, tiled=True)
    preact = jnp.dot(summed, weight, preferred_element_type=jnp.float32)
    activations = jnp.maximum(preact, 0.0).astype(jnp.bfloat16)
    local_grad = lax.dot_general(
        summed, pre_cot, (((0,), (0,)), ((), ())), preferred_element_type=jnp.float32
    )
    total_grad = lax.psum(local_grad, ("blk", "rep"))
    node_total = blocks * rep_count * tile_rows
    grad_weight = total_grad * node_total ** (-0.5)
    return (activations, grad_weight)


MESH = pl.DeviceIdType.MESH
CHUNKS = 1


def fits(mesh):
    blocks, reps = mesh.shape["blk"], mesh.shape["rep"]
    return blocks % 2 == 0 and blocks * reps <= 32


def kernel(blocks, reps, chunks, scale, feat, weight_in, pre_in, count, rowid, cols, vals, act, grad,
           weight, load, onehot, panels, pres, total, part, part_in, s1, r1, s2, r2, r3, r4,
           x_send, x_recv, pre_send, pre_recv, p_send, p_recv,
           g1_send, g1_recv, g2_send, g2_recv, g3_send, g3_recv):
    blk, rep = lax.axis_index("blk"), lax.axis_index("rep")
    tile, width = feat.shape
    part_width = width // chunks
    depth = blocks // 2
    x, z = lax.rem(blk, 2), blk // 2

    loads = [pltpu.make_async_copy(feat.at[:, pl.ds(c * part_width, part_width)], panels.at[c, blk], load.at[c])
             for c in range(chunks)]
    loads.append(pltpu.make_async_copy(pre_in, pres.at[rep], load.at[chunks]))
    loads.append(pltpu.make_async_copy(weight_in, weight, load.at[chunks + 1]))
    for copy in loads:
        copy.start()
    barrier = pltpu.get_barrier_semaphore()
    def greet(to):
        pl.semaphore_signal(barrier, inc=1, device_id=(to, rep), device_id_type=MESH)

    pl.when(z + 1 < depth)(lambda: greet(blk + 2))
    pl.when(z > 0)(lambda: greet(blk - 2))
    greet(blk + 1 - 2 * x)
    for k in range(1, reps):
        pl.semaphore_signal(barrier, inc=1, device_id=(blk, lax.rem(rep + k, reps)), device_id_type=MESH)
    for copy in loads:
        copy.wait()
    ends = (z + 1 < depth).astype(jnp.int32) + (z > 0).astype(jnp.int32)
    pl.semaphore_wait(barrier, reps + ends)

    def remote(src, dst, send, recv, to):
        return pltpu.make_async_remote_copy(
            src_ref=src, dst_ref=dst, send_sem=send, recv_sem=recv, device_id=to, device_id_type=MESH
        )

    targets = (blk + 2, blk - 2, blk + 1 - 2 * x)

    def panel_copy(c, slot, way):
        to = targets[way]
        return remote(panels.at[c, slot], panels.at[c, slot], x_send.at[c, slot, way],
                      x_recv.at[c, slot], (to, rep))

    def order(k):
        low = jnp.minimum(z, depth - 1 - z)
        half = (k + 1) // 2
        near = z - half if k % 2 == 1 else z + half
        far = jnp.where(z < depth - 1 - z, z + (k - low), z - (k - low))
        return jnp.where(k <= 2 * low, near, far)

    def own(c):
        pl.when(z + 1 < depth)(lambda: panel_copy(c, blk, 0).start())
        pl.when(z > 0)(lambda: panel_copy(c, blk, 1).start())
        panel_copy(c, blk, 2).start()

    def build(p, carry):
        rows = lax.broadcasted_iota(jnp.int32, (tile, tile), 0)
        live = count[0, 0, p]
        c0, c1 = cols[0, 0, p, 0], cols[0, 0, p, 1]
        both = vals[0, 0, p, 0].astype(jnp.float32)
        v0, v1 = both[0:1], both[1:2]
        for t in range(reps):
            first = jnp.logical_and(rowid[0, 0, 0, p] == t, live > 0)
            second = jnp.logical_and(rowid[0, 0, 1, p] == t, live > 1)
            value = jnp.where(first, v0, jnp.where(second, v1, 0.0))
            index = jnp.where(first, c0, c1)
            onehot[p, :, t * tile:(t + 1) * tile] = jnp.where(rows == index, value, 0.0).astype(jnp.bfloat16)
        return carry

    def product(c, slot):
        return lax.dot_general(panels[c, slot], onehot[slot], (((0,), (0,)), ((), ())),
                               preferred_element_type=jnp.float32)

    def take(c, slot):
        total[c] += product(c, slot)

    def arrive(c, slot):
        panel_copy(c, slot, 2).wait_recv()

    def step(c, k):
        where = order(k)
        slot = where * 2 + x
        arrive(c, slot)
        pl.when(jnp.logical_and(where < z, z + 1 < depth))(lambda: panel_copy(c, slot, 0).start())
        pl.when(jnp.logical_and(where > z, z > 0))(lambda: panel_copy(c, slot, 1).start())
        panel_copy(c, slot, 2).start()
        take(c, slot)
        last = (z if k == 1 else order(k - 1)) * 2 + 1 - x
        arrive(c, last)
        take(c, last)

    def to_rep(src, dst, send, recv, k):
        return remote(src, dst, send.at[k], recv.at[rep], (blk, lax.rem(rep + k, reps)))

    def from_rep(dst, send, recv, k):
        source = lax.rem(rep + k, reps)
        remote(dst.at[source], dst.at[source], send.at[k], recv.at[source], (blk, source)).wait_recv()
        return source

    def pre_copy(k):
        return to_rep(pres.at[rep], pres.at[rep], pre_send, pre_recv, k)

    def part_copy(c, k):
        return to_rep(part.at[c, lax.rem(rep + k, reps)], part_in.at[c, rep], p_send.at[c], p_recv.at[c], k)

    own(0)
    for k in range(1, reps):
        pre_copy(k).start()
    lax.fori_loop(0, blocks, build, 0)

    grad_rows = []
    for c in range(chunks):
        if c:
            own(c)
        total[c] = product(c, blk)
        for k in range(1, depth):
            step(c, k)
        last = order(depth - 1) * 2 + 1 - x
        arrive(c, last)
        take(c, last)
        for t in range(reps):
            part[c, t] = total[c, :, t * tile:(t + 1) * tile].astype(jnp.bfloat16)
        if c == 0:
            for k in range(1, reps):
                from_rep(pres, pre_send, pre_recv, k)
        rows = jnp.dot(part[c, 0], pres[0], preferred_element_type=jnp.float32)
        for t in range(1, reps):
            rows += jnp.dot(part[c, t], pres[t], preferred_element_type=jnp.float32)
        share = width // reps
        for q in range(part_width // share):
            s1[c * (part_width // share) + q] = rows[q * share:(q + 1) * share]
        if c < chunks - 1:
            for k in range(1, reps):
                part_copy(c, k).start()

    share = width // reps

    def g1_copy(k):
        return to_rep(r1.at[reps + lax.rem(rep + k, reps)], r1.at[rep], g1_send, g1_recv, k)

    for q in range(reps):
        r1[reps + q] = s1[q].astype(jnp.bfloat16)
    for k in range(1, reps):
        g1_copy(k).start()
    for k in range(1, reps):
        part_copy(chunks - 1, k).start()

    mine = s1[rep]
    for k in range(1, reps):
        mine += r1[from_rep(r1, g1_send, g1_recv, k)].astype(jnp.float32)
    piece = share * width // blocks // 128
    lanes = width // 128
    for k in range(blocks):
        s2[k] = mine[(k // lanes) * piece:(k // lanes + 1) * piece,
                     (k % lanes) * 128:(k % lanes + 1) * 128].astype(jnp.bfloat16)

    def to_blk(src, dst, send, recv, k):
        return remote(src, dst, send.at[k], recv.at[blk], (lax.rem(blk + k, blocks), rep))

    def from_blk(dst, send, recv, k):
        source = lax.rem(blk + k, blocks)
        remote(dst.at[source], dst.at[source], send.at[k], recv.at[source], (source, rep)).wait_recv()
        return source

    def g2_copy(k):
        return to_blk(s2.at[lax.rem(blk + k, blocks)], r2.at[blk], g2_send, g2_recv, k)

    for k in range(1, blocks):
        g2_copy(k).start()
    summed = s2[blk].astype(jnp.float32)
    for k in range(1, blocks):
        summed += r2[from_blk(r2, g2_send, g2_recv, k)].astype(jnp.float32)
    r3[blk] = (summed * scale).astype(jnp.bfloat16)

    others = [(i, j) for i in range(blocks) for j in range(reps) if i or j]

    def g3_copy(i, j):
        return remote(r3.at[blk], r4.at[rep, blk], g3_send.at[j, i], g3_recv.at[rep, blk],
                      (lax.rem(blk + i, blocks), lax.rem(rep + j, reps)))

    for i, j in others:
        g3_copy(i, j).start()
    r4[rep, blk] = r3[blk]

    preact = jnp.zeros((tile, width), jnp.float32)
    for c in range(chunks):
        node = part[c, rep].astype(jnp.float32)
        for k in range(1, reps):
            node += part_in[c, from_rep(part_in.at[c], p_send.at[c], p_recv.at[c], k)].astype(jnp.float32)
        preact += lax.dot_general(node.astype(jnp.bfloat16), weight[c * part_width:(c + 1) * part_width],
                                  (((0,), (0,)), ((), ())), preferred_element_type=jnp.float32)
    act[...] = jnp.maximum(preact, 0.0).astype(jnp.bfloat16)

    for c in range(chunks):
        pl.when(z + 1 < depth)(lambda: panel_copy(c, blk, 0).wait_send())
        pl.when(z > 0)(lambda: panel_copy(c, blk, 1).wait_send())
        panel_copy(c, blk, 2).wait_send()
        for k in range(1, depth):
            where = order(k)
            slot = where * 2 + x
            pl.when(jnp.logical_and(where < z, z + 1 < depth))(lambda: panel_copy(c, slot, 0).wait_send())
            pl.when(jnp.logical_and(where > z, z > 0))(lambda: panel_copy(c, slot, 1).wait_send())
            panel_copy(c, slot, 2).wait_send()
        for k in range(1, reps):
            part_copy(c, k).wait_send()
    for k in range(1, reps):
        pre_copy(k).wait_send()
        g1_copy(k).wait_send()
    for k in range(1, blocks):
        g2_copy(k).wait_send()
    for i, j in others:
        b, q = lax.rem(blk + i, blocks), lax.rem(rep + j, reps)
        remote(r4.at[q, b], r4.at[q, b], g3_send.at[j, i], g3_recv.at[q, b], (b, q)).wait_recv()
    grad[...] = r4[...]
    for i, j in others:
        g3_copy(i, j).wait_send()


def fused(features, weight, pre_cot, tile_count, tile_rowid, edge_cols, edge_vals):
    blocks, reps = lax.axis_size("blk"), lax.axis_size("rep")
    tile, width = features.shape
    chunks, part_width = CHUNKS, width // CHUNKS
    share = width // reps
    piece = share * width // blocks // 128
    dma = pltpu.SemaphoreType.DMA
    vmem = pl.BlockSpec(memory_space=pltpu.VMEM)
    hbm = pl.BlockSpec(memory_space=pltpu.HBM)
    smem = pl.BlockSpec(memory_space=pltpu.SMEM)
    bf16 = jnp.bfloat16
    scale = (blocks * reps * tile) ** (-0.5)
    act, pieces = pl.pallas_call(
        functools.partial(kernel, blocks, reps, chunks, scale),
        out_shape=(jax.ShapeDtypeStruct((tile, width), bf16), jax.ShapeDtypeStruct((reps, blocks, piece, 128), bf16)),
        in_specs=[hbm, hbm, hbm, smem, smem, vmem, vmem],
        out_specs=(vmem, vmem),
        scratch_shapes=[
            pltpu.VMEM((width, width), bf16), dma((chunks + 2,)),
            pltpu.VMEM((blocks, tile, reps * tile), bf16),
            pltpu.VMEM((chunks, blocks, tile, part_width), bf16),
            pltpu.VMEM((reps, tile, width), bf16),
            pltpu.VMEM((chunks, part_width, reps * tile), jnp.float32),
            pltpu.VMEM((chunks, reps, part_width, tile), bf16),
            pltpu.VMEM((chunks, reps, part_width, tile), bf16),
            pltpu.VMEM((reps, share, width), jnp.float32),
            pltpu.VMEM((2 * reps, share, width), bf16),
            pltpu.VMEM((blocks, piece, 128), bf16),
            pltpu.VMEM((blocks, piece, 128), bf16),
            pltpu.VMEM((blocks, piece, 128), bf16),
            pltpu.VMEM((reps, blocks, piece, 128), bf16),
            dma((chunks, blocks, 3)), dma((chunks, blocks)), dma((reps,)), dma((reps,)),
            dma((chunks, reps)), dma((chunks, reps)),
            dma((reps,)), dma((reps,)), dma((blocks,)), dma((blocks,)),
            dma((reps, blocks)), dma((reps, blocks)),
        ],
        compiler_params=pltpu.CompilerParams(
            collective_id=0, has_side_effects=True, vmem_limit_bytes=60 * 1024 * 1024
        ),
    )(features, weight, pre_cot, tile_count, tile_rowid.swapaxes(2, 3), edge_cols, edge_vals.swapaxes(3, 4))
    lanes = width // 128
    grid = pieces.reshape(reps, blocks // lanes, lanes, piece, 128).transpose(0, 1, 3, 2, 4)
    return act, grid.reshape(width, width).astype(jnp.float32)


def solution(mesh):
    in_specs = (
        P(("blk", "rep"), None),
        P(),
        P(("blk", "rep"), None),
        P("blk", "rep", None),
        P("blk", "rep", None, None),
        P("blk", "rep", None, None, None, None),
        P("blk", "rep", None, None, None, None),
    )
    out_specs = (P(("blk", "rep"), None), P())
    body = fused if fits(mesh) else shards
    return jax.shard_map(body, mesh=mesh, in_specs=in_specs, out_specs=out_specs, check_vma=False)
```

```python
import functools

import jax
import jax.numpy as jnp
from jax import lax
from jax.experimental import pallas as pl
from jax.experimental.pallas import tpu as pltpu
from jax.sharding import PartitionSpec as P


def shifted(array, axis, by):
    count = lax.axis_size(axis)
    return lax.ppermute(array, axis, [(i, (i + by) % count) for i in range(count)])


def shards(features, weight, pre_cot, tile_count, tile_rowid, edge_cols, edge_vals):
    tile_rows = features.shape[0]
    feat_width = features.shape[1]
    rep_count = lax.axis_size("rep")
    blocks = lax.axis_size("blk")
    home_index = lax.axis_index("blk")
    counts = tile_count.reshape(-1)
    row_ids = tile_rowid.reshape(tile_rowid.shape[2], tile_rowid.shape[3])
    edge_index = edge_cols.reshape(edge_cols.shape[2:])
    edge_weight = edge_vals.reshape(edge_vals.shape[2:])
    slot_count = edge_index.shape[1]
    columns = lax.broadcasted_iota(jnp.int32, (1, 1, 1, tile_rows), 3)
    slot_ids = jnp.arange(slot_count, dtype=jnp.int32)
    zero_weight = jnp.zeros((), jnp.bfloat16)
    totals_start = jnp.zeros((rep_count * tile_rows, feat_width), jnp.float32)

    def apply_panel(totals, panel_now, panel_index):
        index_now = lax.dynamic_index_in_dim(edge_index, panel_index, 0, keepdims=False)
        weight_now = lax.dynamic_index_in_dim(edge_weight, panel_index, 0, keepdims=False)
        dense_tiles = jnp.sum(
            jnp.where(index_now[..., None] == columns, weight_now[..., None], zero_weight), axis=1
        )
        products = jnp.einsum(
            "sij,jf->sif", dense_tiles, panel_now, preferred_element_type=jnp.float32
        )
        live_mask = (slot_ids < counts[panel_index]).astype(jnp.float32)
        slot_rows = lax.dynamic_index_in_dim(row_ids, panel_index, 0, keepdims=False)
        for slot in range(slot_count):
            row_start = slot_rows[slot] * tile_rows
            current = lax.dynamic_slice_in_dim(totals, row_start, tile_rows, 0)
            totals = lax.dynamic_update_slice_in_dim(
                totals, current + products[slot] * live_mask[slot], row_start, 0
            )
        return totals

    totals = apply_panel(totals_start, features, home_index)

    def cycle_turn(turn_index, carry):
        totals_now, panel_now = carry
        panel_now = shifted(panel_now, "blk", 1)
        totals_now = apply_panel(totals_now, panel_now, (home_index - turn_index) % blocks)
        return (totals_now, panel_now)

    totals, _ = lax.fori_loop(1, blocks, cycle_turn, (totals, features))
    summed = lax.psum_scatter(totals.astype(jnp.bfloat16), "rep", scatter_dimension=0, tiled=True)
    preact = jnp.dot(summed, weight, preferred_element_type=jnp.float32)
    activations = jnp.maximum(preact, 0.0).astype(jnp.bfloat16)
    local_grad = lax.dot_general(
        summed, pre_cot, (((0,), (0,)), ((), ())), preferred_element_type=jnp.float32
    )
    total_grad = lax.psum(local_grad, ("blk", "rep"))
    node_total = blocks * rep_count * tile_rows
    grad_weight = total_grad * node_total ** (-0.5)
    return (activations, grad_weight)


MESH = pl.DeviceIdType.MESH
CHUNKS = 1


def fits(mesh):
    blocks, reps = mesh.shape["blk"], mesh.shape["rep"]
    return blocks % 2 == 0 and blocks * reps <= 32


def kernel(blocks, reps, chunks, scale, feat, weight_in, pre_in, count, rowid, cols, vals, act, grad,
           weight, load, onehot, panels, pres, total, part, part_in, s1, s2, r2, r3, r4,
           x_send, x_recv, pre_send, pre_recv, p_send, p_recv,
           g2_send, g2_recv, g3_send, g3_recv):
    blk, rep = lax.axis_index("blk"), lax.axis_index("rep")
    tile, width = feat.shape
    part_width = width // chunks
    depth = blocks // 2
    x, z = lax.rem(blk, 2), blk // 2

    loads = [pltpu.make_async_copy(feat.at[:, pl.ds(c * part_width, part_width)], panels.at[c, blk], load.at[c])
             for c in range(chunks)]
    loads.append(pltpu.make_async_copy(pre_in, pres.at[rep], load.at[chunks]))
    loads.append(pltpu.make_async_copy(weight_in, weight, load.at[chunks + 1]))
    for copy in loads:
        copy.start()
    barrier = pltpu.get_barrier_semaphore()
    def greet(to):
        pl.semaphore_signal(barrier, inc=1, device_id=(to, rep), device_id_type=MESH)

    pl.when(z + 1 < depth)(lambda: greet(blk + 2))
    pl.when(z > 0)(lambda: greet(blk - 2))
    greet(blk + 1 - 2 * x)
    for k in range(1, reps):
        pl.semaphore_signal(barrier, inc=1, device_id=(blk, lax.rem(rep + k, reps)), device_id_type=MESH)
    for copy in loads:
        copy.wait()
    ends = (z + 1 < depth).astype(jnp.int32) + (z > 0).astype(jnp.int32)
    pl.semaphore_wait(barrier, reps + ends)

    def remote(src, dst, send, recv, to):
        return pltpu.make_async_remote_copy(
            src_ref=src, dst_ref=dst, send_sem=send, recv_sem=recv, device_id=to, device_id_type=MESH
        )

    targets = (blk + 2, blk - 2, blk + 1 - 2 * x)

    def panel_copy(c, slot, way):
        to = targets[way]
        return remote(panels.at[c, slot], panels.at[c, slot], x_send.at[c, slot, way],
                      x_recv.at[c, slot], (to, rep))

    def order(k):
        low = jnp.minimum(z, depth - 1 - z)
        half = (k + 1) // 2
        near = z - half if k % 2 == 1 else z + half
        far = jnp.where(z < depth - 1 - z, z + (k - low), z - (k - low))
        return jnp.where(k <= 2 * low, near, far)

    def own(c):
        pl.when(z + 1 < depth)(lambda: panel_copy(c, blk, 0).start())
        pl.when(z > 0)(lambda: panel_copy(c, blk, 1).start())
        panel_copy(c, blk, 2).start()

    def build(p, carry):
        rows = lax.broadcasted_iota(jnp.int32, (tile, tile), 0)
        live = count[0, 0, p]
        c0, c1 = cols[0, 0, p, 0], cols[0, 0, p, 1]
        both = vals[0, 0, p, 0].astype(jnp.float32)
        v0, v1 = both[0:1], both[1:2]
        for t in range(reps):
            first = jnp.logical_and(rowid[0, 0, 0, p] == t, live > 0)
            second = jnp.logical_and(rowid[0, 0, 1, p] == t, live > 1)
            value = jnp.where(first, v0, jnp.where(second, v1, 0.0))
            index = jnp.where(first, c0, c1)
            onehot[p, :, t * tile:(t + 1) * tile] = jnp.where(rows == index, value, 0.0).astype(jnp.bfloat16)
        return carry

    def product(c, slot):
        return lax.dot_general(panels[c, slot], onehot[slot], (((0,), (0,)), ((), ())),
                               preferred_element_type=jnp.float32)

    def take(c, slot):
        total[c] += product(c, slot)

    def arrive(c, slot):
        panel_copy(c, slot, 2).wait_recv()

    def step(c, k):
        where = order(k)
        slot = where * 2 + x
        arrive(c, slot)
        pl.when(jnp.logical_and(where < z, z + 1 < depth))(lambda: panel_copy(c, slot, 0).start())
        pl.when(jnp.logical_and(where > z, z > 0))(lambda: panel_copy(c, slot, 1).start())
        panel_copy(c, slot, 2).start()
        take(c, slot)
        last = (z if k == 1 else order(k - 1)) * 2 + 1 - x
        arrive(c, last)
        take(c, last)

    def to_rep(src, dst, send, recv, k):
        return remote(src, dst, send.at[k], recv.at[rep], (blk, lax.rem(rep + k, reps)))

    def from_rep(dst, send, recv, k):
        source = lax.rem(rep + k, reps)
        remote(dst.at[source], dst.at[source], send.at[k], recv.at[source], (blk, source)).wait_recv()
        return source

    def pre_copy(k):
        return to_rep(pres.at[rep], pres.at[rep], pre_send, pre_recv, k)

    def part_copy(c, k):
        return to_rep(part.at[c, lax.rem(rep + k, reps)], part_in.at[c, rep], p_send.at[c], p_recv.at[c], k)

    own(0)
    for k in range(1, reps):
        pre_copy(k).start()
    lax.fori_loop(0, blocks, build, 0)

    grad_rows = []
    for c in range(chunks):
        if c:
            own(c)
        total[c] = product(c, blk)
        for k in range(1, depth):
            step(c, k)
        last = order(depth - 1) * 2 + 1 - x
        arrive(c, last)
        take(c, last)
        for t in range(reps):
            part[c, t] = total[c, :, t * tile:(t + 1) * tile].astype(jnp.bfloat16)
        if c == 0:
            for k in range(1, reps):
                from_rep(pres, pre_send, pre_recv, k)
        rows = jnp.dot(part[c, 0], pres[0], preferred_element_type=jnp.float32)
        for t in range(1, reps):
            rows += jnp.dot(part[c, t], pres[t], preferred_element_type=jnp.float32)
        share = width // reps
        for q in range(part_width // share):
            s1[c * (part_width // share) + q] = rows[q * share:(q + 1) * share]
        if c < chunks - 1:
            for k in range(1, reps):
                part_copy(c, k).start()

    share = width // reps
    piece = share * width // blocks // 128
    lanes = width // 128
    others = [(i, j) for i in range(blocks) for j in range(reps) if i or j]

    for q in range(reps):
        for k in range(blocks):
            s2[q, k] = s1[q, (k // lanes) * piece:(k // lanes + 1) * piece,
                          (k % lanes) * 128:(k % lanes + 1) * 128].astype(jnp.bfloat16)

    def g2_copy(i, j):
        b, q = lax.rem(blk + i, blocks), lax.rem(rep + j, reps)
        return remote(s2.at[q, b], r2.at[rep, blk], g2_send.at[j, i], g2_recv.at[rep, blk], (b, q))

    for i, j in others:
        g2_copy(i, j).start()
    for k in range(1, reps):
        part_copy(chunks - 1, k).start()
    summed = s2[rep, blk].astype(jnp.float32)
    for i, j in others:
        b, q = lax.rem(blk + i, blocks), lax.rem(rep + j, reps)
        remote(r2.at[q, b], r2.at[q, b], g2_send.at[j, i], g2_recv.at[q, b], (b, q)).wait_recv()
        summed += r2[q, b].astype(jnp.float32)
    r3[blk] = (summed * scale).astype(jnp.bfloat16)

    def g3_copy(i, j):
        return remote(r3.at[blk], r4.at[rep, blk], g3_send.at[j, i], g3_recv.at[rep, blk],
                      (lax.rem(blk + i, blocks), lax.rem(rep + j, reps)))

    for i, j in others:
        g3_copy(i, j).start()
    r4[rep, blk] = r3[blk]

    preact = jnp.zeros((tile, width), jnp.float32)
    for c in range(chunks):
        node = part[c, rep].astype(jnp.float32)
        for k in range(1, reps):
            node += part_in[c, from_rep(part_in.at[c], p_send.at[c], p_recv.at[c], k)].astype(jnp.float32)
        preact += lax.dot_general(node.astype(jnp.bfloat16), weight[c * part_width:(c + 1) * part_width],
                                  (((0,), (0,)), ((), ())), preferred_element_type=jnp.float32)
    act[...] = jnp.maximum(preact, 0.0).astype(jnp.bfloat16)

    for c in range(chunks):
        pl.when(z + 1 < depth)(lambda: panel_copy(c, blk, 0).wait_send())
        pl.when(z > 0)(lambda: panel_copy(c, blk, 1).wait_send())
        panel_copy(c, blk, 2).wait_send()
        for k in range(1, depth):
            where = order(k)
            slot = where * 2 + x
            pl.when(jnp.logical_and(where < z, z + 1 < depth))(lambda: panel_copy(c, slot, 0).wait_send())
            pl.when(jnp.logical_and(where > z, z > 0))(lambda: panel_copy(c, slot, 1).wait_send())
            panel_copy(c, slot, 2).wait_send()
        for k in range(1, reps):
            part_copy(c, k).wait_send()
    for k in range(1, reps):
        pre_copy(k).wait_send()
    for i, j in others:
        g2_copy(i, j).wait_send()
    for i, j in others:
        b, q = lax.rem(blk + i, blocks), lax.rem(rep + j, reps)
        remote(r4.at[q, b], r4.at[q, b], g3_send.at[j, i], g3_recv.at[q, b], (b, q)).wait_recv()
    grad[...] = r4[...]
    for i, j in others:
        g3_copy(i, j).wait_send()


def fused(features, weight, pre_cot, tile_count, tile_rowid, edge_cols, edge_vals):
    blocks, reps = lax.axis_size("blk"), lax.axis_size("rep")
    tile, width = features.shape
    chunks, part_width = CHUNKS, width // CHUNKS
    share = width // reps
    piece = share * width // blocks // 128
    dma = pltpu.SemaphoreType.DMA
    vmem = pl.BlockSpec(memory_space=pltpu.VMEM)
    hbm = pl.BlockSpec(memory_space=pltpu.HBM)
    smem = pl.BlockSpec(memory_space=pltpu.SMEM)
    bf16 = jnp.bfloat16
    scale = (blocks * reps * tile) ** (-0.5)
    act, pieces = pl.pallas_call(
        functools.partial(kernel, blocks, reps, chunks, scale),
        out_shape=(jax.ShapeDtypeStruct((tile, width), bf16), jax.ShapeDtypeStruct((reps, blocks, piece, 128), bf16)),
        in_specs=[hbm, hbm, hbm, smem, smem, vmem, vmem],
        out_specs=(vmem, vmem),
        scratch_shapes=[
            pltpu.VMEM((width, width), bf16), dma((chunks + 2,)),
            pltpu.VMEM((blocks, tile, reps * tile), bf16),
            pltpu.VMEM((chunks, blocks, tile, part_width), bf16),
            pltpu.VMEM((reps, tile, width), bf16),
            pltpu.VMEM((chunks, part_width, reps * tile), jnp.float32),
            pltpu.VMEM((chunks, reps, part_width, tile), bf16),
            pltpu.VMEM((chunks, reps, part_width, tile), bf16),
            pltpu.VMEM((reps, share, width), jnp.float32),
            pltpu.VMEM((reps, blocks, piece, 128), bf16),
            pltpu.VMEM((reps, blocks, piece, 128), bf16),
            pltpu.VMEM((blocks, piece, 128), bf16),
            pltpu.VMEM((reps, blocks, piece, 128), bf16),
            dma((chunks, blocks, 3)), dma((chunks, blocks)), dma((reps,)), dma((reps,)),
            dma((chunks, reps)), dma((chunks, reps)),
            dma((reps, blocks)), dma((reps, blocks)),
            dma((reps, blocks)), dma((reps, blocks)),
        ],
        compiler_params=pltpu.CompilerParams(
            collective_id=0, has_side_effects=True, vmem_limit_bytes=60 * 1024 * 1024
        ),
    )(features, weight, pre_cot, tile_count, tile_rowid.swapaxes(2, 3), edge_cols, edge_vals.swapaxes(3, 4))
    lanes = width // 128
    grid = pieces.reshape(reps, blocks // lanes, lanes, piece, 128).transpose(0, 1, 3, 2, 4)
    return act, grid.reshape(width, width).astype(jnp.float32)


def solution(mesh):
    in_specs = (
        P(("blk", "rep"), None),
        P(),
        P(("blk", "rep"), None),
        P("blk", "rep", None),
        P("blk", "rep", None, None),
        P("blk", "rep", None, None, None, None),
        P("blk", "rep", None, None, None, None),
    )
    out_specs = (P(("blk", "rep"), None), P())
    body = fused if fits(mesh) else shards
    return jax.shard_map(body, mesh=mesh, in_specs=in_specs, out_specs=out_specs, check_vma=False)
```

```python
import functools

import jax
import jax.numpy as jnp
from jax import lax
from jax.experimental import pallas as pl
from jax.experimental.pallas import tpu as pltpu
from jax.sharding import PartitionSpec as P


def shifted(array, axis, by):
    count = lax.axis_size(axis)
    return lax.ppermute(array, axis, [(i, (i + by) % count) for i in range(count)])


def shards(features, weight, pre_cot, tile_count, tile_rowid, edge_cols, edge_vals):
    tile_rows = features.shape[0]
    feat_width = features.shape[1]
    rep_count = lax.axis_size("rep")
    blocks = lax.axis_size("blk")
    home_index = lax.axis_index("blk")
    counts = tile_count.reshape(-1)
    row_ids = tile_rowid.reshape(tile_rowid.shape[2], tile_rowid.shape[3])
    edge_index = edge_cols.reshape(edge_cols.shape[2:])
    edge_weight = edge_vals.reshape(edge_vals.shape[2:])
    slot_count = edge_index.shape[1]
    columns = lax.broadcasted_iota(jnp.int32, (1, 1, 1, tile_rows), 3)
    slot_ids = jnp.arange(slot_count, dtype=jnp.int32)
    zero_weight = jnp.zeros((), jnp.bfloat16)
    totals_start = jnp.zeros((rep_count * tile_rows, feat_width), jnp.float32)

    def apply_panel(totals, panel_now, panel_index):
        index_now = lax.dynamic_index_in_dim(edge_index, panel_index, 0, keepdims=False)
        weight_now = lax.dynamic_index_in_dim(edge_weight, panel_index, 0, keepdims=False)
        dense_tiles = jnp.sum(
            jnp.where(index_now[..., None] == columns, weight_now[..., None], zero_weight), axis=1
        )
        products = jnp.einsum(
            "sij,jf->sif", dense_tiles, panel_now, preferred_element_type=jnp.float32
        )
        live_mask = (slot_ids < counts[panel_index]).astype(jnp.float32)
        slot_rows = lax.dynamic_index_in_dim(row_ids, panel_index, 0, keepdims=False)
        for slot in range(slot_count):
            row_start = slot_rows[slot] * tile_rows
            current = lax.dynamic_slice_in_dim(totals, row_start, tile_rows, 0)
            totals = lax.dynamic_update_slice_in_dim(
                totals, current + products[slot] * live_mask[slot], row_start, 0
            )
        return totals

    totals = apply_panel(totals_start, features, home_index)

    def cycle_turn(turn_index, carry):
        totals_now, panel_now = carry
        panel_now = shifted(panel_now, "blk", 1)
        totals_now = apply_panel(totals_now, panel_now, (home_index - turn_index) % blocks)
        return (totals_now, panel_now)

    totals, _ = lax.fori_loop(1, blocks, cycle_turn, (totals, features))
    summed = lax.psum_scatter(totals.astype(jnp.bfloat16), "rep", scatter_dimension=0, tiled=True)
    preact = jnp.dot(summed, weight, preferred_element_type=jnp.float32)
    activations = jnp.maximum(preact, 0.0).astype(jnp.bfloat16)
    local_grad = lax.dot_general(
        summed, pre_cot, (((0,), (0,)), ((), ())), preferred_element_type=jnp.float32
    )
    total_grad = lax.psum(local_grad, ("blk", "rep"))
    node_total = blocks * rep_count * tile_rows
    grad_weight = total_grad * node_total ** (-0.5)
    return (activations, grad_weight)


MESH = pl.DeviceIdType.MESH
CHUNKS = 1
HALVES = 2


def fits(mesh):
    blocks, reps = mesh.shape["blk"], mesh.shape["rep"]
    return blocks % 2 == 0 and blocks * reps <= 32


def kernel(blocks, reps, chunks, scale, feat, weight_in, pre_in, count, rowid, cols, vals, act, grad,
           weight, load, onehot, panels, pres, total, part, part_in, s1, s2, r2, r3, r4,
           x_send, x_recv, pre_send, pre_recv, p_send, p_recv,
           g2_send, g2_recv, g3_send, g3_recv):
    blk, rep = lax.axis_index("blk"), lax.axis_index("rep")
    tile, width = feat.shape
    part_width = width // chunks
    depth = blocks // 2
    x, z = lax.rem(blk, 2), blk // 2

    loads = [pltpu.make_async_copy(feat.at[:, pl.ds(c * part_width, part_width)], panels.at[c, blk], load.at[c])
             for c in range(chunks)]
    loads.append(pltpu.make_async_copy(pre_in, pres.at[rep], load.at[chunks]))
    loads.append(pltpu.make_async_copy(weight_in, weight, load.at[chunks + 1]))
    for copy in loads:
        copy.start()
    barrier = pltpu.get_barrier_semaphore()
    def greet(to):
        pl.semaphore_signal(barrier, inc=1, device_id=(to, rep), device_id_type=MESH)

    pl.when(z + 1 < depth)(lambda: greet(blk + 2))
    pl.when(z > 0)(lambda: greet(blk - 2))
    greet(blk + 1 - 2 * x)
    for k in range(1, reps):
        pl.semaphore_signal(barrier, inc=1, device_id=(blk, lax.rem(rep + k, reps)), device_id_type=MESH)
    for copy in loads:
        copy.wait()
    ends = (z + 1 < depth).astype(jnp.int32) + (z > 0).astype(jnp.int32)
    pl.semaphore_wait(barrier, reps + ends)

    def remote(src, dst, send, recv, to):
        return pltpu.make_async_remote_copy(
            src_ref=src, dst_ref=dst, send_sem=send, recv_sem=recv, device_id=to, device_id_type=MESH
        )

    targets = (blk + 2, blk - 2, blk + 1 - 2 * x)

    def panel_copy(c, slot, way, half):
        rows = panels.at[c, slot, pl.ds(half * (tile // HALVES), tile // HALVES)]
        return remote(rows, rows, x_send.at[c, slot, way, half],
                      x_recv.at[c, slot, half], (targets[way], rep))

    def order(k):
        low = jnp.minimum(z, depth - 1 - z)
        half = (k + 1) // 2
        near = z - half if k % 2 == 1 else z + half
        far = jnp.where(z < depth - 1 - z, z + (k - low), z - (k - low))
        return jnp.where(k <= 2 * low, near, far)

    def own(c):
        for h in range(HALVES):
            pl.when(z + 1 < depth)(lambda: panel_copy(c, blk, 0, h).start())
            pl.when(z > 0)(lambda: panel_copy(c, blk, 1, h).start())
            panel_copy(c, blk, 2, h).start()

    def build(p, carry):
        rows = lax.broadcasted_iota(jnp.int32, (tile, tile), 0)
        live = count[0, 0, p]
        c0, c1 = cols[0, 0, p, 0], cols[0, 0, p, 1]
        both = vals[0, 0, p, 0].astype(jnp.float32)
        v0, v1 = both[0:1], both[1:2]
        for t in range(reps):
            first = jnp.logical_and(rowid[0, 0, 0, p] == t, live > 0)
            second = jnp.logical_and(rowid[0, 0, 1, p] == t, live > 1)
            value = jnp.where(first, v0, jnp.where(second, v1, 0.0))
            index = jnp.where(first, c0, c1)
            onehot[p, :, t * tile:(t + 1) * tile] = jnp.where(rows == index, value, 0.0).astype(jnp.bfloat16)
        return carry

    def product(c, slot):
        return lax.dot_general(panels[c, slot], onehot[slot], (((0,), (0,)), ((), ())),
                               preferred_element_type=jnp.float32)

    def take(c, slot):
        total[c] += product(c, slot)

    def arrive(c, slot):
        for h in range(HALVES):
            panel_copy(c, slot, 2, h).wait_recv()

    def step(c, k):
        where = order(k)
        slot = where * 2 + x
        for h in range(HALVES):
            panel_copy(c, slot, 2, h).wait_recv()
            pl.when(jnp.logical_and(where < z, z + 1 < depth))(lambda: panel_copy(c, slot, 0, h).start())
            pl.when(jnp.logical_and(where > z, z > 0))(lambda: panel_copy(c, slot, 1, h).start())
            panel_copy(c, slot, 2, h).start()
        take(c, slot)
        last = (z if k == 1 else order(k - 1)) * 2 + 1 - x
        arrive(c, last)
        take(c, last)

    def to_rep(src, dst, send, recv, k):
        return remote(src, dst, send.at[k], recv.at[rep], (blk, lax.rem(rep + k, reps)))

    def from_rep(dst, send, recv, k):
        source = lax.rem(rep + k, reps)
        remote(dst.at[source], dst.at[source], send.at[k], recv.at[source], (blk, source)).wait_recv()
        return source

    def pre_copy(k):
        return to_rep(pres.at[rep], pres.at[rep], pre_send, pre_recv, k)

    def part_copy(c, k):
        return to_rep(part.at[c, lax.rem(rep + k, reps)], part_in.at[c, rep], p_send.at[c], p_recv.at[c], k)

    own(0)
    for k in range(1, reps):
        pre_copy(k).start()
    lax.fori_loop(0, blocks, build, 0)

    grad_rows = []
    for c in range(chunks):
        if c:
            own(c)
        total[c] = product(c, blk)
        for k in range(1, depth):
            step(c, k)
        last = order(depth - 1) * 2 + 1 - x
        arrive(c, last)
        take(c, last)
        for t in range(reps):
            part[c, t] = total[c, :, t * tile:(t + 1) * tile].astype(jnp.bfloat16)
        if c == 0:
            for k in range(1, reps):
                from_rep(pres, pre_send, pre_recv, k)
        rows = jnp.dot(part[c, 0], pres[0], preferred_element_type=jnp.float32)
        for t in range(1, reps):
            rows += jnp.dot(part[c, t], pres[t], preferred_element_type=jnp.float32)
        share = width // reps
        for q in range(part_width // share):
            s1[c * (part_width // share) + q] = rows[q * share:(q + 1) * share]
        if c < chunks - 1:
            for k in range(1, reps):
                part_copy(c, k).start()

    share = width // reps
    piece = share * width // blocks // 128
    lanes = width // 128
    others = [(i, j) for i in range(blocks) for j in range(reps) if i or j]

    for q in range(reps):
        for k in range(blocks):
            s2[q, k] = s1[q, (k // lanes) * piece:(k // lanes + 1) * piece,
                          (k % lanes) * 128:(k % lanes + 1) * 128].astype(jnp.bfloat16)

    def g2_copy(i, j):
        b, q = lax.rem(blk + i, blocks), lax.rem(rep + j, reps)
        return remote(s2.at[q, b], r2.at[rep, blk], g2_send.at[j, i], g2_recv.at[rep, blk], (b, q))

    for i, j in others:
        g2_copy(i, j).start()
    for k in range(1, reps):
        part_copy(chunks - 1, k).start()
    summed = s2[rep, blk].astype(jnp.float32)
    for i, j in others:
        b, q = lax.rem(blk + i, blocks), lax.rem(rep + j, reps)
        remote(r2.at[q, b], r2.at[q, b], g2_send.at[j, i], g2_recv.at[q, b], (b, q)).wait_recv()
        summed += r2[q, b].astype(jnp.float32)
    r3[blk] = (summed * scale).astype(jnp.bfloat16)

    def g3_copy(i, j):
        return remote(r3.at[blk], r4.at[rep, blk], g3_send.at[j, i], g3_recv.at[rep, blk],
                      (lax.rem(blk + i, blocks), lax.rem(rep + j, reps)))

    for i, j in others:
        g3_copy(i, j).start()
    r4[rep, blk] = r3[blk]

    preact = jnp.zeros((tile, width), jnp.float32)
    for c in range(chunks):
        node = part[c, rep].astype(jnp.float32)
        for k in range(1, reps):
            node += part_in[c, from_rep(part_in.at[c], p_send.at[c], p_recv.at[c], k)].astype(jnp.float32)
        preact += lax.dot_general(node.astype(jnp.bfloat16), weight[c * part_width:(c + 1) * part_width],
                                  (((0,), (0,)), ((), ())), preferred_element_type=jnp.float32)
    act[...] = jnp.maximum(preact, 0.0).astype(jnp.bfloat16)

    for c in range(chunks):
        for h in range(HALVES):
            pl.when(z + 1 < depth)(lambda: panel_copy(c, blk, 0, h).wait_send())
            pl.when(z > 0)(lambda: panel_copy(c, blk, 1, h).wait_send())
            panel_copy(c, blk, 2, h).wait_send()
            for k in range(1, depth):
                where = order(k)
                slot = where * 2 + x
                pl.when(jnp.logical_and(where < z, z + 1 < depth))(lambda: panel_copy(c, slot, 0, h).wait_send())
                pl.when(jnp.logical_and(where > z, z > 0))(lambda: panel_copy(c, slot, 1, h).wait_send())
                panel_copy(c, slot, 2, h).wait_send()
        for k in range(1, reps):
            part_copy(c, k).wait_send()
    for k in range(1, reps):
        pre_copy(k).wait_send()
    for i, j in others:
        g2_copy(i, j).wait_send()
    for i, j in others:
        b, q = lax.rem(blk + i, blocks), lax.rem(rep + j, reps)
        remote(r4.at[q, b], r4.at[q, b], g3_send.at[j, i], g3_recv.at[q, b], (b, q)).wait_recv()
    grad[...] = r4[...]
    for i, j in others:
        g3_copy(i, j).wait_send()


def fused(features, weight, pre_cot, tile_count, tile_rowid, edge_cols, edge_vals):
    blocks, reps = lax.axis_size("blk"), lax.axis_size("rep")
    tile, width = features.shape
    chunks, part_width = CHUNKS, width // CHUNKS
    share = width // reps
    piece = share * width // blocks // 128
    dma = pltpu.SemaphoreType.DMA
    vmem = pl.BlockSpec(memory_space=pltpu.VMEM)
    hbm = pl.BlockSpec(memory_space=pltpu.HBM)
    smem = pl.BlockSpec(memory_space=pltpu.SMEM)
    bf16 = jnp.bfloat16
    scale = (blocks * reps * tile) ** (-0.5)
    act, pieces = pl.pallas_call(
        functools.partial(kernel, blocks, reps, chunks, scale),
        out_shape=(jax.ShapeDtypeStruct((tile, width), bf16), jax.ShapeDtypeStruct((reps, blocks, piece, 128), bf16)),
        in_specs=[hbm, hbm, hbm, smem, smem, vmem, vmem],
        out_specs=(vmem, vmem),
        scratch_shapes=[
            pltpu.VMEM((width, width), bf16), dma((chunks + 2,)),
            pltpu.VMEM((blocks, tile, reps * tile), bf16),
            pltpu.VMEM((chunks, blocks, tile, part_width), bf16),
            pltpu.VMEM((reps, tile, width), bf16),
            pltpu.VMEM((chunks, part_width, reps * tile), jnp.float32),
            pltpu.VMEM((chunks, reps, part_width, tile), bf16),
            pltpu.VMEM((chunks, reps, part_width, tile), bf16),
            pltpu.VMEM((reps, share, width), jnp.float32),
            pltpu.VMEM((reps, blocks, piece, 128), bf16),
            pltpu.VMEM((reps, blocks, piece, 128), bf16),
            pltpu.VMEM((blocks, piece, 128), bf16),
            pltpu.VMEM((reps, blocks, piece, 128), bf16),
            dma((chunks, blocks, 3, HALVES)), dma((chunks, blocks, HALVES)), dma((reps,)), dma((reps,)),
            dma((chunks, reps)), dma((chunks, reps)),
            dma((reps, blocks)), dma((reps, blocks)),
            dma((reps, blocks)), dma((reps, blocks)),
        ],
        compiler_params=pltpu.CompilerParams(
            collective_id=0, has_side_effects=True, vmem_limit_bytes=60 * 1024 * 1024
        ),
    )(features, weight, pre_cot, tile_count, tile_rowid.swapaxes(2, 3), edge_cols, edge_vals.swapaxes(3, 4))
    lanes = width // 128
    grid = pieces.reshape(reps, blocks // lanes, lanes, piece, 128).transpose(0, 1, 3, 2, 4)
    return act, grid.reshape(width, width).astype(jnp.float32)


def solution(mesh):
    in_specs = (
        P(("blk", "rep"), None),
        P(),
        P(("blk", "rep"), None),
        P("blk", "rep", None),
        P("blk", "rep", None, None),
        P("blk", "rep", None, None, None, None),
        P("blk", "rep", None, None, None, None),
    )
    out_specs = (P(("blk", "rep"), None), P())
    body = fused if fits(mesh) else shards
    return jax.shard_map(body, mesh=mesh, in_specs=in_specs, out_specs=out_specs, check_vma=False)
```

```python
import functools

import jax
import jax.numpy as jnp
from jax import lax
from jax.experimental import pallas as pl
from jax.experimental.pallas import tpu as pltpu
from jax.sharding import PartitionSpec as P


def shifted(array, axis, by):
    count = lax.axis_size(axis)
    return lax.ppermute(array, axis, [(i, (i + by) % count) for i in range(count)])


def shards(features, weight, pre_cot, tile_count, tile_rowid, edge_cols, edge_vals):
    tile_rows = features.shape[0]
    feat_width = features.shape[1]
    rep_count = lax.axis_size("rep")
    blocks = lax.axis_size("blk")
    home_index = lax.axis_index("blk")
    counts = tile_count.reshape(-1)
    row_ids = tile_rowid.reshape(tile_rowid.shape[2], tile_rowid.shape[3])
    edge_index = edge_cols.reshape(edge_cols.shape[2:])
    edge_weight = edge_vals.reshape(edge_vals.shape[2:])
    slot_count = edge_index.shape[1]
    columns = lax.broadcasted_iota(jnp.int32, (1, 1, 1, tile_rows), 3)
    slot_ids = jnp.arange(slot_count, dtype=jnp.int32)
    zero_weight = jnp.zeros((), jnp.bfloat16)
    totals_start = jnp.zeros((rep_count * tile_rows, feat_width), jnp.float32)

    def apply_panel(totals, panel_now, panel_index):
        index_now = lax.dynamic_index_in_dim(edge_index, panel_index, 0, keepdims=False)
        weight_now = lax.dynamic_index_in_dim(edge_weight, panel_index, 0, keepdims=False)
        dense_tiles = jnp.sum(
            jnp.where(index_now[..., None] == columns, weight_now[..., None], zero_weight), axis=1
        )
        products = jnp.einsum(
            "sij,jf->sif", dense_tiles, panel_now, preferred_element_type=jnp.float32
        )
        live_mask = (slot_ids < counts[panel_index]).astype(jnp.float32)
        slot_rows = lax.dynamic_index_in_dim(row_ids, panel_index, 0, keepdims=False)
        for slot in range(slot_count):
            row_start = slot_rows[slot] * tile_rows
            current = lax.dynamic_slice_in_dim(totals, row_start, tile_rows, 0)
            totals = lax.dynamic_update_slice_in_dim(
                totals, current + products[slot] * live_mask[slot], row_start, 0
            )
        return totals

    totals = apply_panel(totals_start, features, home_index)

    def cycle_turn(turn_index, carry):
        totals_now, panel_now = carry
        panel_now = shifted(panel_now, "blk", 1)
        totals_now = apply_panel(totals_now, panel_now, (home_index - turn_index) % blocks)
        return (totals_now, panel_now)

    totals, _ = lax.fori_loop(1, blocks, cycle_turn, (totals, features))
    summed = lax.psum_scatter(totals.astype(jnp.bfloat16), "rep", scatter_dimension=0, tiled=True)
    preact = jnp.dot(summed, weight, preferred_element_type=jnp.float32)
    activations = jnp.maximum(preact, 0.0).astype(jnp.bfloat16)
    local_grad = lax.dot_general(
        summed, pre_cot, (((0,), (0,)), ((), ())), preferred_element_type=jnp.float32
    )
    total_grad = lax.psum(local_grad, ("blk", "rep"))
    node_total = blocks * rep_count * tile_rows
    grad_weight = total_grad * node_total ** (-0.5)
    return (activations, grad_weight)


MESH = pl.DeviceIdType.MESH
CHUNKS = 1
HALVES = 4


def fits(mesh):
    blocks, reps = mesh.shape["blk"], mesh.shape["rep"]
    return blocks % 2 == 0 and blocks * reps <= 32


def kernel(blocks, reps, chunks, scale, feat, weight_in, pre_in, count, rowid, cols, vals, act, grad,
           weight, load, onehot, panels, pres, total, part, part_in, s1, s2, r2, r3, r4,
           x_send, x_recv, pre_send, pre_recv, p_send, p_recv,
           g2_send, g2_recv, g3_send, g3_recv):
    blk, rep = lax.axis_index("blk"), lax.axis_index("rep")
    tile, width = feat.shape
    part_width = width // chunks
    depth = blocks // 2
    x, z = lax.rem(blk, 2), blk // 2

    loads = [pltpu.make_async_copy(feat.at[:, pl.ds(c * part_width, part_width)], panels.at[c, blk], load.at[c])
             for c in range(chunks)]
    loads.append(pltpu.make_async_copy(pre_in, pres.at[rep], load.at[chunks]))
    loads.append(pltpu.make_async_copy(weight_in, weight, load.at[chunks + 1]))
    for copy in loads:
        copy.start()
    barrier = pltpu.get_barrier_semaphore()
    def greet(to):
        pl.semaphore_signal(barrier, inc=1, device_id=(to, rep), device_id_type=MESH)

    pl.when(z + 1 < depth)(lambda: greet(blk + 2))
    pl.when(z > 0)(lambda: greet(blk - 2))
    greet(blk + 1 - 2 * x)
    for k in range(1, reps):
        pl.semaphore_signal(barrier, inc=1, device_id=(blk, lax.rem(rep + k, reps)), device_id_type=MESH)
    for copy in loads:
        copy.wait()
    ends = (z + 1 < depth).astype(jnp.int32) + (z > 0).astype(jnp.int32)
    pl.semaphore_wait(barrier, reps + ends)

    def remote(src, dst, send, recv, to):
        return pltpu.make_async_remote_copy(
            src_ref=src, dst_ref=dst, send_sem=send, recv_sem=recv, device_id=to, device_id_type=MESH
        )

    targets = (blk + 2, blk - 2, blk + 1 - 2 * x)

    def panel_copy(c, slot, way, half):
        rows = panels.at[c, slot, pl.ds(half * (tile // HALVES), tile // HALVES)]
        return remote(rows, rows, x_send.at[c, slot, way, half],
                      x_recv.at[c, slot, half], (targets[way], rep))

    def order(k):
        low = jnp.minimum(z, depth - 1 - z)
        half = (k + 1) // 2
        near = z - half if k % 2 == 1 else z + half
        far = jnp.where(z < depth - 1 - z, z + (k - low), z - (k - low))
        return jnp.where(k <= 2 * low, near, far)

    def own(c):
        for h in range(HALVES):
            pl.when(z + 1 < depth)(lambda: panel_copy(c, blk, 0, h).start())
            pl.when(z > 0)(lambda: panel_copy(c, blk, 1, h).start())
            panel_copy(c, blk, 2, h).start()

    def build(p, carry):
        rows = lax.broadcasted_iota(jnp.int32, (tile, tile), 0)
        live = count[0, 0, p]
        c0, c1 = cols[0, 0, p, 0], cols[0, 0, p, 1]
        both = vals[0, 0, p, 0].astype(jnp.float32)
        v0, v1 = both[0:1], both[1:2]
        for t in range(reps):
            first = jnp.logical_and(rowid[0, 0, 0, p] == t, live > 0)
            second = jnp.logical_and(rowid[0, 0, 1, p] == t, live > 1)
            value = jnp.where(first, v0, jnp.where(second, v1, 0.0))
            index = jnp.where(first, c0, c1)
            onehot[p, :, t * tile:(t + 1) * tile] = jnp.where(rows == index, value, 0.0).astype(jnp.bfloat16)
        return carry

    def product(c, slot):
        return lax.dot_general(panels[c, slot], onehot[slot], (((0,), (0,)), ((), ())),
                               preferred_element_type=jnp.float32)

    def take(c, slot):
        total[c] += product(c, slot)

    def arrive(c, slot):
        for h in range(HALVES):
            panel_copy(c, slot, 2, h).wait_recv()

    def step(c, k):
        where = order(k)
        slot = where * 2 + x
        for h in range(HALVES):
            panel_copy(c, slot, 2, h).wait_recv()
            pl.when(jnp.logical_and(where < z, z + 1 < depth))(lambda: panel_copy(c, slot, 0, h).start())
            pl.when(jnp.logical_and(where > z, z > 0))(lambda: panel_copy(c, slot, 1, h).start())
            panel_copy(c, slot, 2, h).start()
        take(c, slot)
        last = (z if k == 1 else order(k - 1)) * 2 + 1 - x
        arrive(c, last)
        take(c, last)

    def to_rep(src, dst, send, recv, k):
        return remote(src, dst, send.at[k], recv.at[rep], (blk, lax.rem(rep + k, reps)))

    def from_rep(dst, send, recv, k):
        source = lax.rem(rep + k, reps)
        remote(dst.at[source], dst.at[source], send.at[k], recv.at[source], (blk, source)).wait_recv()
        return source

    def pre_copy(k):
        return to_rep(pres.at[rep], pres.at[rep], pre_send, pre_recv, k)

    def part_copy(c, k):
        return to_rep(part.at[c, lax.rem(rep + k, reps)], part_in.at[c, rep], p_send.at[c], p_recv.at[c], k)

    own(0)
    for k in range(1, reps):
        pre_copy(k).start()
    lax.fori_loop(0, blocks, build, 0)

    grad_rows = []
    for c in range(chunks):
        if c:
            own(c)
        total[c] = product(c, blk)
        for k in range(1, depth):
            step(c, k)
        last = order(depth - 1) * 2 + 1 - x
        arrive(c, last)
        take(c, last)
        for t in range(reps):
            part[c, t] = total[c, :, t * tile:(t + 1) * tile].astype(jnp.bfloat16)
        if c == 0:
            for k in range(1, reps):
                from_rep(pres, pre_send, pre_recv, k)
        rows = jnp.dot(part[c, 0], pres[0], preferred_element_type=jnp.float32)
        for t in range(1, reps):
            rows += jnp.dot(part[c, t], pres[t], preferred_element_type=jnp.float32)
        share = width // reps
        for q in range(part_width // share):
            s1[c * (part_width // share) + q] = rows[q * share:(q + 1) * share]
        if c < chunks - 1:
            for k in range(1, reps):
                part_copy(c, k).start()

    share = width // reps
    piece = share * width // blocks // 128
    lanes = width // 128
    others = [(i, j) for i in range(blocks) for j in range(reps) if i or j]

    for q in range(reps):
        for k in range(blocks):
            s2[q, k] = s1[q, (k // lanes) * piece:(k // lanes + 1) * piece,
                          (k % lanes) * 128:(k % lanes + 1) * 128].astype(jnp.bfloat16)

    def g2_copy(i, j):
        b, q = lax.rem(blk + i, blocks), lax.rem(rep + j, reps)
        return remote(s2.at[q, b], r2.at[rep, blk], g2_send.at[j, i], g2_recv.at[rep, blk], (b, q))

    for i, j in others:
        g2_copy(i, j).start()
    for k in range(1, reps):
        part_copy(chunks - 1, k).start()
    summed = s2[rep, blk].astype(jnp.float32)
    for i, j in others:
        b, q = lax.rem(blk + i, blocks), lax.rem(rep + j, reps)
        remote(r2.at[q, b], r2.at[q, b], g2_send.at[j, i], g2_recv.at[q, b], (b, q)).wait_recv()
        summed += r2[q, b].astype(jnp.float32)
    r3[blk] = (summed * scale).astype(jnp.bfloat16)

    def g3_copy(i, j):
        return remote(r3.at[blk], r4.at[rep, blk], g3_send.at[j, i], g3_recv.at[rep, blk],
                      (lax.rem(blk + i, blocks), lax.rem(rep + j, reps)))

    for i, j in others:
        g3_copy(i, j).start()
    r4[rep, blk] = r3[blk]

    preact = jnp.zeros((tile, width), jnp.float32)
    for c in range(chunks):
        node = part[c, rep].astype(jnp.float32)
        for k in range(1, reps):
            node += part_in[c, from_rep(part_in.at[c], p_send.at[c], p_recv.at[c], k)].astype(jnp.float32)
        preact += lax.dot_general(node.astype(jnp.bfloat16), weight[c * part_width:(c + 1) * part_width],
                                  (((0,), (0,)), ((), ())), preferred_element_type=jnp.float32)
    act[...] = jnp.maximum(preact, 0.0).astype(jnp.bfloat16)

    for c in range(chunks):
        for h in range(HALVES):
            pl.when(z + 1 < depth)(lambda: panel_copy(c, blk, 0, h).wait_send())
            pl.when(z > 0)(lambda: panel_copy(c, blk, 1, h).wait_send())
            panel_copy(c, blk, 2, h).wait_send()
            for k in range(1, depth):
                where = order(k)
                slot = where * 2 + x
                pl.when(jnp.logical_and(where < z, z + 1 < depth))(lambda: panel_copy(c, slot, 0, h).wait_send())
                pl.when(jnp.logical_and(where > z, z > 0))(lambda: panel_copy(c, slot, 1, h).wait_send())
                panel_copy(c, slot, 2, h).wait_send()
        for k in range(1, reps):
            part_copy(c, k).wait_send()
    for k in range(1, reps):
        pre_copy(k).wait_send()
    for i, j in others:
        g2_copy(i, j).wait_send()
    for i, j in others:
        b, q = lax.rem(blk + i, blocks), lax.rem(rep + j, reps)
        remote(r4.at[q, b], r4.at[q, b], g3_send.at[j, i], g3_recv.at[q, b], (b, q)).wait_recv()
    grad[...] = r4[...]
    for i, j in others:
        g3_copy(i, j).wait_send()


def fused(features, weight, pre_cot, tile_count, tile_rowid, edge_cols, edge_vals):
    blocks, reps = lax.axis_size("blk"), lax.axis_size("rep")
    tile, width = features.shape
    chunks, part_width = CHUNKS, width // CHUNKS
    share = width // reps
    piece = share * width // blocks // 128
    dma = pltpu.SemaphoreType.DMA
    vmem = pl.BlockSpec(memory_space=pltpu.VMEM)
    hbm = pl.BlockSpec(memory_space=pltpu.HBM)
    smem = pl.BlockSpec(memory_space=pltpu.SMEM)
    bf16 = jnp.bfloat16
    scale = (blocks * reps * tile) ** (-0.5)
    act, pieces = pl.pallas_call(
        functools.partial(kernel, blocks, reps, chunks, scale),
        out_shape=(jax.ShapeDtypeStruct((tile, width), bf16), jax.ShapeDtypeStruct((reps, blocks, piece, 128), bf16)),
        in_specs=[hbm, hbm, hbm, smem, smem, vmem, vmem],
        out_specs=(vmem, vmem),
        scratch_shapes=[
            pltpu.VMEM((width, width), bf16), dma((chunks + 2,)),
            pltpu.VMEM((blocks, tile, reps * tile), bf16),
            pltpu.VMEM((chunks, blocks, tile, part_width), bf16),
            pltpu.VMEM((reps, tile, width), bf16),
            pltpu.VMEM((chunks, part_width, reps * tile), jnp.float32),
            pltpu.VMEM((chunks, reps, part_width, tile), bf16),
            pltpu.VMEM((chunks, reps, part_width, tile), bf16),
            pltpu.VMEM((reps, share, width), jnp.float32),
            pltpu.VMEM((reps, blocks, piece, 128), bf16),
            pltpu.VMEM((reps, blocks, piece, 128), bf16),
            pltpu.VMEM((blocks, piece, 128), bf16),
            pltpu.VMEM((reps, blocks, piece, 128), bf16),
            dma((chunks, blocks, 3, HALVES)), dma((chunks, blocks, HALVES)), dma((reps,)), dma((reps,)),
            dma((chunks, reps)), dma((chunks, reps)),
            dma((reps, blocks)), dma((reps, blocks)),
            dma((reps, blocks)), dma((reps, blocks)),
        ],
        compiler_params=pltpu.CompilerParams(
            collective_id=0, has_side_effects=True, vmem_limit_bytes=60 * 1024 * 1024
        ),
    )(features, weight, pre_cot, tile_count, tile_rowid.swapaxes(2, 3), edge_cols, edge_vals.swapaxes(3, 4))
    lanes = width // 128
    grid = pieces.reshape(reps, blocks // lanes, lanes, piece, 128).transpose(0, 1, 3, 2, 4)
    return act, grid.reshape(width, width).astype(jnp.float32)


def solution(mesh):
    in_specs = (
        P(("blk", "rep"), None),
        P(),
        P(("blk", "rep"), None),
        P("blk", "rep", None),
        P("blk", "rep", None, None),
        P("blk", "rep", None, None, None, None),
        P("blk", "rep", None, None, None, None),
    )
    out_specs = (P(("blk", "rep"), None), P())
    body = fused if fits(mesh) else shards
    return jax.shard_map(body, mesh=mesh, in_specs=in_specs, out_specs=out_specs, check_vma=False)
```
